32 devices in a mesh: hist: 4 (over x, core), cand: 4 (over z), fsdp: 2 (over y).
Axes of the slice: x: 2, y: 2, z: 4, core: 2. Of those that a mesh axis runs over, the one named last changes fastest.
Arguments:
- candidates: bfloat16 [256, 4, 1024], P(('hist', 'cand'), 'fsdp'), may hold values from -6 to 6
- cand_items: int32 [256, 4], replicated, may hold values from 0 to 2047, as said below
- hist_keys: bfloat16 [4, 4096, 1024], P('fsdp', 'hist'), may hold values from -6 to 6
- hist_values: bfloat16 [4, 4096, 1024], P('fsdp', 'hist'), may hold values from -6 to 6
- hist_items: int32 [4, 4096], P('fsdp', 'hist'), may hold values from 0 to 2047
- hist_buckets: int32 [4, 4096], P('fsdp', 'hist'), may hold values from 0 to 127
- lengths: int32 [4], P('fsdp'), may hold values from 1024 to 4096, as said below
- norm_gain: float32 [1024], replicated, may hold values from 0.5 to 1.5
- in_weight: bfloat16 [1024, 4096], P(None, 'fsdp'), may hold values from -0.1875 to 0.1875
- bias_table: float32 [128, 16], replicated, may hold values from -4 to 4
- out_weight: bfloat16 [1024, 1024], P(None, 'fsdp'), may hold values from -0.1875 to 0.1875
Outputs:
- scored: bfloat16 [256, 4, 1024], P(('hist', 'cand'), 'fsdp')
The draws below stay inside these ranges and needn't reach their ends.
Inputs may be any that keep to these rules, and one draw needn't show every extreme that they name: `lengths`: history length of each user; one user of every draw has all 4096 positions. `cand_items`: item ids of the candidates, from the same catalogue as the history.
All inputs are finite; a program needn't handle non-finite values.
Results may differ from the reference program's by a relative error of at most 0.013.
Values may be sent and summed in bfloat16 or wider, within the bound.
A program may use at most 128 MiB of HBM per device.

```python
import math
import jax
import jax.numpy as jnp
from jax import lax

D = 1024
H = 16
HD = 1024
NB = 128
ITEMS = 2048
HIST_DEV = 1024
USERS = 4
CANDS = 256
HIST = 4096


def item_draw(key, out_shape, salt_value):
    catalogue = jax.random.permutation(jax.random.fold_in(key, 71), ITEMS).astype(jnp.int32)
    depth_bits = ITEMS.bit_length() - 1
    level_draw = jax.random.randint(jax.random.fold_in(key, salt_value), out_shape, 0, depth_bits + 1)
    upper_bound = jnp.left_shift(jnp.int32(1), level_draw.astype(jnp.int32))
    rank_draw = jax.random.randint(jax.random.fold_in(key, salt_value + 1), out_shape, 0, upper_bound)
    return catalogue[rank_draw].astype(jnp.int32)


def draw_cand_items(key, part):
    return item_draw(key, (CANDS, USERS), 13)


def draw_hist_items(key, part):
    return item_draw(key, (USERS, HIST), 29)


def draw_lengths(key, part):
    spread = jax.random.randint(jax.random.fold_in(key, 5), (USERS,), HIST // 4, HIST + 1)
    longest = jax.random.randint(jax.random.fold_in(key, 6), (), 0, USERS)
    return jnp.where(jnp.arange(USERS) == longest, HIST, spread).astype(jnp.int32)


def with_ends(result, key, smallest, largest):
    longest = result.shape.index(max(result.shape))
    spots = []
    for shift in (0, 1):
        where = [jax.random.randint(jax.random.fold_in(key, axis), (), 0, length) for axis, length in enumerate(result.shape)]
        where[longest] = (where[longest] + shift) % result.shape[longest]
        spots.append(tuple(where))
    return result.at[spots[0]].set(smallest).at[spots[1]].set(largest)


def steps_of(stream_key, shape, shards, least, top_value):
    def one(position, blocks):
        heights = jax.random.uniform(jax.random.fold_in(jax.random.fold_in(stream_key, 6), position), (blocks,), jnp.float32, least / len(shards), top_value / len(shards))
        return jnp.repeat(jnp.exp(heights), shape[position] // blocks).reshape((-1,) + (1,) * (len(shape) - position - 1))

    factor_of = one(*shards[0])
    for cut in shards[1:]:
        factor_of = factor_of * one(*cut)
    return factor_of


def normal_values(own_key, shape, width, limit, shards=(), held_as=jnp.bfloat16):
    values = width * jax.random.normal(own_key, shape, jnp.float32)
    if shards:
        values = values * steps_of(own_key, shape, shards, -0.22, 0.18)
    return jnp.clip(values, -limit, limit).astype(held_as)


def setup_inputs(seed: int = 0) -> dict:
    arg_keys = jax.random.split(jax.random.key(seed), 12)
    candidates = normal_values(arg_keys[0], (CANDS, USERS, D), 1.0, 6.0, ((0, 16), (1, 2)))
    cand_items = draw_cand_items(jax.random.fold_in(arg_keys[11], 71), 0)
    hist_keys = normal_values(arg_keys[2], (USERS, HIST, HD), 1.0, 6.0, ((0, 2), (1, 4)))
    hist_values = normal_values(arg_keys[3], (USERS, HIST, HD), 1.0, 6.0, ((0, 2), (1, 4)))
    hist_items = draw_hist_items(jax.random.fold_in(arg_keys[11], 71), 0)
    hist_buckets = with_ends(jax.random.randint(arg_keys[5], (USERS, HIST), 0, NB), jax.random.fold_in(arg_keys[5], 1), 0, NB - 1).astype(jnp.int32)
    lengths = draw_lengths(jax.random.fold_in(arg_keys[11], 71), 0)
    norm_gain = jnp.clip(jax.random.uniform(arg_keys[7], (D,), jnp.float32, 0.5, 1.5), 0.5, 1.5)
    in_weight = normal_values(arg_keys[8], (D, 4 * HD), D ** -0.5, 0.1875, ((1, 2),))
    bias_table = normal_values(arg_keys[9], (NB, H), 1.0, 4.0, (), jnp.float32)
    out_weight = normal_values(arg_keys[10], (HD, D), HD ** -0.5, 0.1875, ((1, 2),))
    return {"candidates": candidates, "cand_items": cand_items, "hist_keys": hist_keys, "hist_values": hist_values, "hist_items": hist_items, "hist_buckets": hist_buckets, "lengths": lengths, "norm_gain": norm_gain, "in_weight": in_weight, "bias_table": bias_table, "out_weight": out_weight}


def layer_norm(values_in, epsilon):
    center = values_in - lax.optimization_barrier(jnp.mean(values_in, axis=-1, keepdims=True))
    spread = lax.optimization_barrier(jnp.mean(center * center, axis=-1, keepdims=True))
    return center * lax.rsqrt(spread + epsilon)

def reference(candidates, cand_items, hist_keys, hist_values, hist_items, hist_buckets, lengths, norm_gain, in_weight, bias_table, out_weight):
    cand_total, member_total, model_width = candidates.shape
    head_count = bias_table.shape[1]
    inner_width = out_weight.shape[0]
    head_dim = inner_width // head_count
    score_scale = head_dim ** (-0.5)
    normed = (layer_norm(candidates.astype(jnp.float32), 1e-05) * norm_gain).astype(jnp.bfloat16)
    projected = jax.nn.silu(jnp.dot(normed.reshape(cand_total * member_total, model_width), in_weight, preferred_element_type=jnp.float32))
    projected = projected.astype(jnp.bfloat16).reshape(cand_total, member_total, 4 * inner_width)
    gate_part = projected[:, :, :inner_width]
    value_part = projected[:, :, inner_width:2 * inner_width]
    query_part = projected[:, :, 2 * inner_width:3 * inner_width]
    key_part = projected[:, :, 3 * inner_width:]
    inv_len = 1.0 / (lengths.astype(jnp.float32) + 1.0)
    query_heads = query_part.astype(jnp.float32).reshape(cand_total, member_total, head_count, head_dim)
    key_heads = key_part.astype(jnp.float32).reshape(cand_total, member_total, head_count, head_dim)
    self_weight = jax.nn.silu(lax.optimization_barrier(jnp.sum(query_heads * key_heads, axis=-1)) * score_scale + bias_table[0][None, None, :]) * inv_len[None, :, None]
    self_term = (self_weight[..., None] * value_part.astype(jnp.float32).reshape(cand_total, member_total, head_count, head_dim)).reshape(cand_total, member_total, inner_width)
    block_rows = math.gcd(cand_total, 512)
    key_block = HIST_DEV
    hist_len = hist_keys.shape[1]
    positions = jnp.arange(hist_len, dtype=jnp.int32).reshape(-1, key_block)

    def per_member(packed):
        member_q, member_ids, member_k, member_v, member_items, member_buckets, member_len, member_inv = packed
        bias_rows = bias_table[member_buckets].T.reshape(head_count, -1, key_block).transpose(1, 0, 2)
        key_blocks = member_k.astype(jnp.float32).reshape(-1, key_block, head_count, head_dim)
        value_blocks = member_v.astype(jnp.float32).reshape(-1, key_block, head_count, head_dim)
        item_blocks = member_items.reshape(-1, key_block)
        query_blocks = member_q.astype(jnp.float32).reshape(-1, block_rows, head_count, head_dim)
        id_blocks = member_ids.reshape(-1, block_rows)

        def per_block(block_pair):
            query_rows, row_ids = block_pair

            def key_step(running, pieces):
                key_rows, value_rows, bias_piece, item_piece, pos_piece = pieces
                scores = jnp.einsum('qhd,khd->qhk', query_rows, key_rows) * score_scale + bias_piece[None]
                keep_mask = (pos_piece[None, :] < member_len) & (item_piece[None, :] != row_ids[:, None])
                weights = jnp.where(keep_mask[:, None, :], jax.nn.silu(scores) * member_inv, 0.0)
                weights = lax.optimization_barrier(weights.astype(jnp.bfloat16)).astype(jnp.float32)
                return (running + jnp.einsum('qhk,khd->qhd', weights, value_rows), None)
            start_sum = jnp.zeros((block_rows, head_count, head_dim), jnp.float32)
            summed, _ = lax.scan(key_step, start_sum, (key_blocks, value_blocks, bias_rows, item_blocks, positions))
            return summed.reshape(block_rows, inner_width)
        return lax.map(per_block, (query_blocks, id_blocks)).reshape(cand_total, inner_width)
    attended = lax.map(per_member, (query_part.transpose(1, 0, 2), cand_items.T, hist_keys, hist_values, hist_items, hist_buckets, lengths, inv_len))
    attended = attended.transpose(1, 0, 2) + self_term
    mixed = (layer_norm(attended, 1e-05) * gate_part.astype(jnp.float32)).astype(jnp.bfloat16)
    branch = jnp.dot(mixed.reshape(cand_total * member_total, inner_width), out_weight, preferred_element_type=jnp.float32)
    return (candidates.astype(jnp.float32) + branch.reshape(cand_total, member_total, model_width)).astype(jnp.bfloat16)
```

```python
import functools

import jax
import jax.numpy as jnp
from jax import lax
from jax.experimental import pallas as pl
from jax.experimental.pallas import tpu as pltpu
from jax.sharding import PartitionSpec as P

MESH = pl.DeviceIdType.MESH
F32 = jnp.float32
BF16 = jnp.bfloat16
NT = (((1,), (1,)), ((), ()))


def half_silu(u):
    return u + u * jnp.tanh(u)


def layer_norm(x):
    c = x - jnp.mean(x, axis=-1, keepdims=True)
    return c * lax.rsqrt(jnp.mean(c * c, axis=-1, keepdims=True) + 1e-05)


def kernel(
    hist_n,
    cand_n,
    cand_ref,
    ids_ref,
    keys_hbm,
    vals_hbm,
    items_ref,
    buckets_ref,
    len_ref,
    gain_ref,
    inw_hbm,
    table_ref,
    outw_hbm,
    out_ref,
    inw,
    outw,
    keys,
    vals,
    x_buf,
    proj,
    psend,
    gq,
    part,
    recv,
    hbias,
    keep,
    mix,
    branch,
    bsend,
    loc_sem,
    a_send,
    a_recv,
    c_send,
    c_recv,
    d_send,
    d_recv,
    f_send,
    f_recv,
    m_send,
    m_recv,
    b_send,
    b_recv,
):
    hist = lax.axis_index("hist")
    cand = lax.axis_index("cand")
    fsdp = lax.axis_index("fsdp")
    other = 1 - fsdp
    members, cdev, width = cand_ref.shape
    heads, buckets = table_ref.shape
    inner = part.shape[-1]
    rows_own = members * cdev
    key_n = keys.shape[1]
    rows = hist_n * cdev
    hd = inner // heads
    group = 256 // hd
    gcols = group * hd
    group_n = inner // gcols

    def remote(src, dst, ssem, rsem, **where):
        return pltpu.make_async_remote_copy(
            src_ref=src, dst_ref=dst, send_sem=ssem, recv_sem=rsem, device_id=where, device_id_type=MESH
        )

    loc = [pltpu.make_async_copy(inw_hbm, inw, loc_sem.at[0])]
    for m in range(members):
        loc.append(pltpu.make_async_copy(keys_hbm.at[m], keys.at[m], loc_sem.at[1 + 2 * m]))
        loc.append(pltpu.make_async_copy(vals_hbm.at[m], vals.at[m], loc_sem.at[2 + 2 * m]))
    loc.append(pltpu.make_async_copy(outw_hbm, outw, loc_sem.at[1 + 2 * members]))

    barrier = pltpu.get_barrier_semaphore()
    peers = [lax.rem(hist + o, hist_n) for o in range(1, hist_n)]
    for peer in peers:
        pl.semaphore_signal(barrier, inc=1, device_id={"hist": peer}, device_id_type=MESH)
    pl.semaphore_signal(barrier, inc=1, device_id={"fsdp": other}, device_id_type=MESH)
    for copy in loc:
        copy.start()
    x = cand_ref[...].astype(F32).reshape(rows_own, width)
    x_buf[0] = (layer_norm(x) * gain_ref[...]).astype(BF16)
    pl.semaphore_wait(barrier, hist_n)

    a_copy = remote(x_buf.at[0], x_buf.at[1], a_send, a_recv, fsdp=other)
    a_copy.start()

    table = table_ref[...]
    t_hi = table.astype(BF16)
    rest = table - t_hi.astype(F32)
    t_mid = rest.astype(BF16)
    t_lo = (rest - t_mid.astype(F32)).astype(BF16)
    t3 = jnp.concatenate([t_hi, t_mid, t_lo], axis=0)
    for m in range(members):
        one_hot = (
            lax.broadcasted_iota(jnp.int32, (buckets, key_n), 0) == buckets_ref[m : m + 1, :]
        )
        b3 = jnp.dot(t3, one_hot.astype(F32).astype(BF16), preferred_element_type=F32)
        hbias[m] = 0.5 * (b3[:heads] + b3[heads : 2 * heads] + b3[2 * heads :])

    loc[0].wait()
    a_copy.wait()
    xs = x_buf[...].reshape(2 * rows_own, width)

    def project(p):
        u = 0.5 * jnp.dot(xs, inw[:, p * inner : (p + 1) * inner], preferred_element_type=F32)
        y = half_silu(u).astype(BF16)
        proj[2 * fsdp + p] = y[:rows_own].reshape(members, cdev, inner)
        psend[p] = y[rows_own:].reshape(members, cdev, inner)
        copy = remote(psend.at[p], proj.at[2 * fsdp + p], c_send.at[p], c_recv.at[p], fsdp=other)
        copy.start()
        return copy

    c0 = project(0)
    c1 = project(1)
    c0.wait()
    d_copies = [
        remote(proj.at[2], gq.at[hist], d_send.at[o], d_recv.at[o], hist=peer)
        for o, peer in enumerate(peers)
    ]
    for copy in d_copies:
        copy.start()
    gq[hist] = proj[2]

    lane_ids = lax.broadcasted_iota(jnp.int32, (cdev, ids_ref.shape[1]), 1)
    place = hist * key_n + lax.broadcasted_iota(jnp.int32, (1, key_n), 1)
    for m in range(members):
        length = jnp.full((1, key_n), len_ref[m], jnp.int32)
        scale = jnp.where(place < length, 1.0 / (length.astype(F32) + 1.0), 0.0)

        def fill(h, carry):
            block = ids_ref[pl.ds(pl.multiple_of((h * cand_n + cand) * cdev, cdev), cdev), :]
            mine = jnp.sum(
                jnp.where(lane_ids == fsdp * members + m, block, 0), axis=1, keepdims=True
            )
            keep[m, h] = jnp.where(mine != items_ref[m : m + 1, :], scale, 0.0)
            return carry

        lax.fori_loop(0, hist_n, fill, 0)

    for copy in d_copies:
        copy.wait()

    hb = 4 if hist_n % 4 == 0 else 1
    rb = hb * cdev
    lane_head = lax.broadcasted_iota(jnp.int32, (rb, gcols), 1) // hd
    f_copies = []
    chunk = min(key_n, 512)
    for m in range(members):
        loc[1 + 2 * m].wait()
        loc[2 + 2 * m].wait()

        def step(i, carry):
            r = i // group_n
            g = i % group_n
            cols = pl.ds(pl.multiple_of(g * gcols, gcols), gcols)
            hs = pl.ds(r * hb, hb)
            q = gq[hs, m, :, cols].reshape(rb, gcols).astype(F32) * (0.5 * hd ** (-0.5))
            q4 = jnp.concatenate(
                [jnp.where(lane_head == h, q, 0.0).astype(BF16) for h in range(group)], axis=0
            )
            total = jnp.zeros((group * rb, gcols), F32)
            for j in range(0, key_n, chunk):
                s = lax.dot_general(
                    q4, keys[m, pl.ds(j, chunk), cols], NT, preferred_element_type=F32
                )
                kp = keep[m, hs, :, pl.ds(j, chunk)].reshape(rb, chunk)
                ws = []
                for h in range(group):
                    u = s[h * rb : (h + 1) * rb] + hbias[m, pl.ds(g * group + h, 1), pl.ds(j, chunk)]
                    ws.append((half_silu(u) * kp).astype(BF16))
                total += jnp.dot(
                    jnp.concatenate(ws, axis=0),
                    vals[m, pl.ds(j, chunk), cols],
                    preferred_element_type=F32,
                )
            summed = jnp.where(lane_head == 0, total[:rb], 0.0)
            for h in range(1, group):
                summed += jnp.where(lane_head == h, total[h * rb : (h + 1) * rb], 0.0)
            part[m, hs, :, cols] = summed.astype(BF16).reshape(hb, cdev, gcols)
            return carry

        lax.fori_loop(0, (hist_n // hb) * group_n, step, 0)
        for o, peer in enumerate(peers):
            copy = remote(
                part.at[m, peer], recv.at[m, hist], f_send.at[m, o], f_recv.at[m, o], hist=peer
            )
            copy.start()
            f_copies.append(copy)

    c1.wait()
    blk = (
        lax.broadcasted_iota(jnp.int32, (gcols, gcols), 0) // hd
        == lax.broadcasted_iota(jnp.int32, (gcols, gcols), 1) // hd
    ).astype(F32).astype(BF16)
    prod = proj[2].astype(F32).reshape(rows_own, inner) * proj[3].astype(F32).reshape(rows_own, inner)
    p_hi = prod.astype(BF16)
    p_lo = (prod - p_hi.astype(F32)).astype(BF16)
    dots = jnp.concatenate(
        [
            jnp.dot(p_hi[:, c : c + gcols], blk, preferred_element_type=F32)
            + jnp.dot(p_lo[:, c : c + gcols], blk, preferred_element_type=F32)
            for c in range(0, inner, gcols)
        ],
        axis=1,
    )
    lane = lax.broadcasted_iota(jnp.int32, (heads, inner), 1) // hd
    bias0 = jnp.sum(
        jnp.where(lax.broadcasted_iota(jnp.int32, (heads, inner), 0) == lane, table[:, 0:1], 0.0),
        axis=0,
        keepdims=True,
    )
    own = half_silu(dots * (0.5 * hd ** (-0.5)) + 0.5 * bias0)
    own = own * proj[1].astype(F32).reshape(rows_own, inner)
    inv = jnp.concatenate(
        [1.0 / (jnp.full((cdev, inner), len_ref[m], jnp.int32).astype(F32) + 1.0) for m in range(members)],
        axis=0,
    )
    attended = own * inv
    for m in range(members):
        recv[m, hist] = part[m, hist]
    for copy in f_copies:
        copy.wait()
    attended += jnp.sum(recv[...].astype(F32), axis=1).reshape(rows_own, inner)
    mix[0] = (layer_norm(attended) * proj[0].astype(F32).reshape(rows_own, inner)).astype(BF16)
    m_copy = remote(mix.at[0], mix.at[1], m_send, m_recv, fsdp=other)
    m_copy.start()
    loc[-1].wait()
    m_copy.wait()
    bsend[...] = jnp.dot(mix[1], outw[...], preferred_element_type=F32)
    b_copy = remote(bsend, branch.at[fsdp], b_send, b_recv, fsdp=other)
    b_copy.start()
    branch[fsdp] = jnp.dot(mix[0], outw[...], preferred_element_type=F32)
    b_copy.wait()
    full = jnp.concatenate([branch[0], branch[1]], axis=1)
    x = cand_ref[...].astype(F32).reshape(rows_own, width)
    out_ref[...] = (x + full).astype(BF16).reshape(members, cdev, width)


def body(
    hist_n,
    cand_n,
    candidates,
    cand_items,
    hist_keys,
    hist_values,
    hist_items,
    hist_buckets,
    lengths,
    norm_gain,
    in_weight,
    bias_table,
    out_weight,
):
    cdev, members, width = candidates.shape
    key_n = hist_keys.shape[1]
    inner = out_weight.shape[0]
    heads = bias_table.shape[1]
    own = members * cdev
    vmem = pl.BlockSpec(memory_space=pltpu.VMEM)
    hbm = pl.BlockSpec(memory_space=pl.ANY)
    smem = pl.BlockSpec(memory_space=pltpu.SMEM)
    dma = pltpu.SemaphoreType.DMA
    peers = max(hist_n - 1, 1)
    out = pl.pallas_call(
        functools.partial(kernel, hist_n, cand_n),
        out_shape=jax.ShapeDtypeStruct((members, cdev, width), BF16),
        in_specs=[vmem, vmem, hbm, hbm, vmem, vmem, smem, vmem, hbm, vmem, hbm],
        out_specs=vmem,
        scratch_shapes=[
            pltpu.VMEM(in_weight.shape, BF16),
            pltpu.VMEM(out_weight.shape, BF16),
            pltpu.VMEM(hist_keys.shape, BF16),
            pltpu.VMEM(hist_values.shape, BF16),
            pltpu.VMEM((2, own, width), BF16),
            pltpu.VMEM((4, members, cdev, inner), BF16),
            pltpu.VMEM((2, members, cdev, inner), BF16),
            pltpu.VMEM((hist_n, members, cdev, inner), BF16),
            pltpu.VMEM((members, hist_n, cdev, inner), BF16),
            pltpu.VMEM((members, hist_n, cdev, inner), BF16),
            pltpu.VMEM((members, heads, key_n), F32),
            pltpu.VMEM((members, hist_n, cdev, key_n), F32),
            pltpu.VMEM((2, own, inner), BF16),
            pltpu.VMEM((2, own, out_weight.shape[1]), F32),
            pltpu.VMEM((own, out_weight.shape[1]), F32),
            dma((2 + 2 * members,)),
            dma(()),
            dma(()),
            dma((2,)),
            dma((2,)),
            dma((peers,)),
            dma((peers,)),
            dma((members, peers)),
            dma((members, peers)),
            dma(()),
            dma(()),
            dma(()),
            dma(()),
        ],
        compiler_params=pltpu.CompilerParams(
            collective_id=0, has_side_effects=True, vmem_limit_bytes=56 * 1024 * 1024
        ),
    )(
        candidates.transpose(1, 0, 2),
        cand_items,
        hist_keys,
        hist_values,
        hist_items,
        hist_buckets,
        lengths,
        norm_gain.reshape(1, width),
        in_weight,
        bias_table.T,
        out_weight,
    )
    return out.transpose(1, 0, 2)


def solution(mesh):
    in_specs = (
        P(("hist", "cand"), "fsdp", None),
        P(),
        P("fsdp", "hist", None),
        P("fsdp", "hist", None),
        P("fsdp", "hist"),
        P("fsdp", "hist"),
        P("fsdp"),
        P(),
        P(None, "fsdp"),
        P(),
        P(None, "fsdp"),
    )
    out_specs = P(("hist", "cand"), "fsdp", None)
    return jax.shard_map(
        functools.partial(body, mesh.shape["hist"], mesh.shape["cand"]),
        mesh=mesh,
        in_specs=in_specs,
        out_specs=out_specs,
        check_vma=False,
    )
```

```python
import functools

import jax
import jax.numpy as jnp
from jax import lax
from jax.experimental import pallas as pl
from jax.experimental.pallas import tpu as pltpu
from jax.sharding import PartitionSpec as P

MESH = pl.DeviceIdType.MESH
F32 = jnp.float32
BF16 = jnp.bfloat16
NT = (((1,), (1,)), ((), ()))


def half_silu(u):
    return u + u * jnp.tanh(u)


def layer_norm(x):
    c = x - jnp.mean(x, axis=-1, keepdims=True)
    return c * lax.rsqrt(jnp.mean(c * c, axis=-1, keepdims=True) + 1e-05)


def kernel(
    hist_n,
    cand_n,
    cand_ref,
    ids_ref,
    keys_hbm,
    vals_hbm,
    items_ref,
    buckets_ref,
    len_ref,
    gain_ref,
    inw_hbm,
    table_ref,
    outw_hbm,
    out_ref,
    inw,
    outw,
    keys,
    vals,
    x_buf,
    proj,
    psend,
    gq,
    part,
    recv,
    hbias,
    keep,
    loc_sem,
    a_send,
    a_recv,
    c_send,
    c_recv,
    d_send,
    d_recv,
    f_send,
    f_recv,
    o_send,
    o_recv,
    s_send,
    s_recv,
):
    hist = lax.axis_index("hist")
    cand = lax.axis_index("cand")
    fsdp = lax.axis_index("fsdp")
    other = 1 - fsdp
    cdev, members, width = cand_ref.shape
    heads, buckets = table_ref.shape
    inner = part.shape[-1]
    rows_own = members * cdev
    key_n = keys.shape[1]
    hd = inner // heads
    group = 256 // hd
    gcols = group * hd
    group_n = inner // gcols

    def remote(src, dst, ssem, rsem, **where):
        return pltpu.make_async_remote_copy(
            src_ref=src, dst_ref=dst, send_sem=ssem, recv_sem=rsem, device_id=where, device_id_type=MESH
        )

    loc = [pltpu.make_async_copy(inw_hbm, inw, loc_sem.at[0])]
    for m in range(members):
        loc.append(pltpu.make_async_copy(keys_hbm.at[m], keys.at[m], loc_sem.at[1 + 2 * m]))
        loc.append(pltpu.make_async_copy(vals_hbm.at[m], vals.at[m], loc_sem.at[2 + 2 * m]))
    w_copy = pltpu.make_async_copy(outw_hbm, outw.at[fsdp], loc_sem.at[1 + 2 * members])
    loc.insert(1, w_copy)

    barrier = pltpu.get_barrier_semaphore()
    peers = [lax.rem(hist + o, hist_n) for o in range(1, hist_n)]
    for peer in peers:
        pl.semaphore_signal(barrier, inc=1, device_id={"hist": peer}, device_id_type=MESH)
    pl.semaphore_signal(barrier, inc=1, device_id={"fsdp": other}, device_id_type=MESH)
    for copy in loc:
        copy.start()
    x3 = cand_ref[...].astype(F32)
    x = jnp.concatenate([x3[:, m, :] for m in range(members)], axis=0)
    x_buf[0] = (layer_norm(x) * gain_ref[...]).astype(BF16)
    pl.semaphore_wait(barrier, hist_n)

    a_copy = remote(x_buf.at[0], x_buf.at[1], a_send, a_recv, fsdp=other)
    a_copy.start()

    table = table_ref[...]
    t_hi = table.astype(BF16)
    rest = table - t_hi.astype(F32)
    t_mid = rest.astype(BF16)
    t_lo = (rest - t_mid.astype(F32)).astype(BF16)
    t3 = jnp.concatenate([t_hi, t_mid, t_lo], axis=0)
    for m in range(members):
        one_hot = (
            lax.broadcasted_iota(jnp.int32, (buckets, key_n), 0) == buckets_ref[m : m + 1, :]
        )
        b3 = jnp.dot(t3, one_hot.astype(F32).astype(BF16), preferred_element_type=F32)
        hbias[m] = 0.5 * (b3[:heads] + b3[heads : 2 * heads] + b3[2 * heads :])

    loc[0].wait()
    a_copy.wait()
    xs = x_buf[...].reshape(2 * rows_own, width)

    def project(p):
        u = 0.5 * jnp.dot(xs, inw[:, p * inner : (p + 1) * inner], preferred_element_type=F32)
        y = half_silu(u).astype(BF16)
        psend[p] = y[rows_own:].reshape(members, cdev, inner)
        copies = []
        for m in range(members):
            copy = remote(
                psend.at[p, m],
                proj.at[2 * fsdp + p, m],
                c_send.at[p, m],
                c_recv.at[p, m],
                fsdp=other,
            )
            copy.start()
            copies.append(copy)
        proj[2 * fsdp + p] = y[:rows_own].reshape(members, cdev, inner)
        return copies

    c0 = project(0)

    lane_ids = lax.broadcasted_iota(jnp.int32, (cdev, ids_ref.shape[1]), 1)
    row_ids = lax.broadcasted_iota(jnp.int32, (cdev, ids_ref.shape[1]), 0)
    place = hist * key_n + lax.broadcasted_iota(jnp.int32, (1, key_n), 1)
    for m in range(members):
        length = jnp.full((1, key_n), len_ref[m], jnp.int32)
        scale = jnp.where(place < length, 1.0 / (length.astype(F32) + 1.0), 0.0)

        def fill(h, carry):
            ids = ids_ref[pl.ds(fsdp * members + m, 1), :]
            mine = jnp.sum(
                jnp.where(lane_ids == row_ids + (h * cand_n + cand) * cdev, ids, 0),
                axis=1,
                keepdims=True,
            )
            keep[m, h] = jnp.where(mine != items_ref[m : m + 1, :], scale, 0.0)
            return carry

        lax.fori_loop(0, hist_n, fill, 0)

    d_copies = []
    for m in range(members):
        c0[m].wait()
        d_copies.append(
            [
                remote(
                    proj.at[2, m], gq.at[m, hist], d_send.at[m, o], d_recv.at[m, o], hist=peer
                )
                for o, peer in enumerate(peers)
            ]
        )
        for copy in d_copies[m]:
            copy.start()
        gq[m, hist] = proj[2, m]
    c1 = project(1)

    depth = inner // 2
    rows = pl.ds(pl.multiple_of(lax.rem(hist, 2) * depth, depth), depth)
    w_copy.wait()
    o_copy = remote(outw.at[fsdp, rows], outw.at[fsdp, rows], o_send, o_recv, fsdp=other)
    o_copy.start()

    hb = 4 if hist_n % 4 == 0 else 1
    rb = hb * cdev
    lane_head = lax.broadcasted_iota(jnp.int32, (rb, gcols), 1) // hd
    f_copies = []
    chunk = min(key_n, 512)
    for m in range(members):
        loc[2 + 2 * m].wait()
        loc[3 + 2 * m].wait()
        for copy in d_copies[m]:
            copy.wait()

        def step(i, carry):
            r = i // group_n
            g = i % group_n
            cols = pl.ds(pl.multiple_of(g * gcols, gcols), gcols)
            hs = pl.ds(r * hb, hb)
            q = gq[m, hs, :, cols].reshape(rb, gcols).astype(F32) * (0.5 * hd ** (-0.5))
            q4 = jnp.concatenate(
                [jnp.where(lane_head == h, q, 0.0).astype(BF16) for h in range(group)], axis=0
            )
            total = jnp.zeros((group * rb, gcols), F32)
            for j in range(0, key_n, chunk):
                s = lax.dot_general(
                    q4, keys[m, pl.ds(j, chunk), cols], NT, preferred_element_type=F32
                )
                kp = keep[m, hs, :, pl.ds(j, chunk)].reshape(rb, chunk)
                ws = []
                for h in range(group):
                    u = s[h * rb : (h + 1) * rb] + hbias[m, pl.ds(g * group + h, 1), pl.ds(j, chunk)]
                    ws.append((half_silu(u) * kp).astype(BF16))
                total += jnp.dot(
                    jnp.concatenate(ws, axis=0),
                    vals[m, pl.ds(j, chunk), cols],
                    preferred_element_type=F32,
                )
            summed = jnp.where(lane_head == 0, total[:rb], 0.0)
            for h in range(1, group):
                summed += jnp.where(lane_head == h, total[h * rb : (h + 1) * rb], 0.0)
            part[m, hs, :, cols] = summed.astype(BF16).reshape(hb, cdev, gcols)
            return carry

        lax.fori_loop(0, (hist_n // hb) * group_n, step, 0)
        for o, peer in enumerate(peers):
            copy = remote(
                part.at[m, peer], recv.at[m, hist], f_send.at[m, o], f_recv.at[m, o], hist=peer
            )
            copy.start()
            f_copies.append(copy)

    o_copy.wait()
    sibling = hist + 1 - 2 * lax.rem(hist, 2)
    s_copy = remote(outw.at[other, rows], outw.at[other, rows], s_send, s_recv, hist=sibling)
    s_copy.start()
    for copy in c1:
        copy.wait()
    blk = (
        lax.broadcasted_iota(jnp.int32, (gcols, gcols), 0) // hd
        == lax.broadcasted_iota(jnp.int32, (gcols, gcols), 1) // hd
    ).astype(F32).astype(BF16)
    prod = proj[2].astype(F32).reshape(rows_own, inner) * proj[3].astype(F32).reshape(rows_own, inner)
    p_hi = prod.astype(BF16)
    p_lo = (prod - p_hi.astype(F32)).astype(BF16)
    dots = jnp.concatenate(
        [
            jnp.dot(p_hi[:, c : c + gcols], blk, preferred_element_type=F32)
            + jnp.dot(p_lo[:, c : c + gcols], blk, preferred_element_type=F32)
            for c in range(0, inner, gcols)
        ],
        axis=1,
    )
    lane = lax.broadcasted_iota(jnp.int32, (heads, inner), 1) // hd
    bias0 = jnp.sum(
        jnp.where(lax.broadcasted_iota(jnp.int32, (heads, inner), 0) == lane, table[:, 0:1], 0.0),
        axis=0,
        keepdims=True,
    )
    own = half_silu(dots * (0.5 * hd ** (-0.5)) + 0.5 * bias0)
    own = own * proj[1].astype(F32).reshape(rows_own, inner)
    inv = jnp.concatenate(
        [1.0 / (jnp.full((cdev, inner), len_ref[m], jnp.int32).astype(F32) + 1.0) for m in range(members)],
        axis=0,
    )
    attended = own * inv
    for m in range(members):
        recv[m, hist] = part[m, hist]
    for copy in f_copies:
        copy.wait()
    attended += jnp.sum(recv[...].astype(F32), axis=1).reshape(rows_own, inner)
    mixed = (layer_norm(attended) * proj[0].astype(F32).reshape(rows_own, inner)).astype(BF16)
    s_copy.wait()
    full = jnp.concatenate(
        [jnp.dot(mixed, outw[f], preferred_element_type=F32) for f in range(2)], axis=1
    )
    x3 = cand_ref[...].astype(F32)
    x = jnp.concatenate([x3[:, m, :] for m in range(members)], axis=0)
    out_ref[...] = (x + full).astype(BF16).reshape(members, cdev, width)


def body(
    hist_n,
    cand_n,
    candidates,
    cand_items,
    hist_keys,
    hist_values,
    hist_items,
    hist_buckets,
    lengths,
    norm_gain,
    in_weight,
    bias_table,
    out_weight,
):
    cdev, members, width = candidates.shape
    key_n = hist_keys.shape[1]
    inner = out_weight.shape[0]
    heads = bias_table.shape[1]
    own = members * cdev
    vmem = pl.BlockSpec(memory_space=pltpu.VMEM)
    hbm = pl.BlockSpec(memory_space=pl.ANY)
    smem = pl.BlockSpec(memory_space=pltpu.SMEM)
    dma = pltpu.SemaphoreType.DMA
    peers = max(hist_n - 1, 1)
    out = pl.pallas_call(
        functools.partial(kernel, hist_n, cand_n),
        out_shape=jax.ShapeDtypeStruct((members, cdev, width), BF16),
        in_specs=[vmem, vmem, hbm, hbm, vmem, vmem, smem, vmem, hbm, vmem, hbm],
        out_specs=vmem,
        scratch_shapes=[
            pltpu.VMEM(in_weight.shape, BF16),
            pltpu.VMEM((2,) + out_weight.shape, BF16),
            pltpu.VMEM(hist_keys.shape, BF16),
            pltpu.VMEM(hist_values.shape, BF16),
            pltpu.VMEM((2, own, width), BF16),
            pltpu.VMEM((4, members, cdev, inner), BF16),
            pltpu.VMEM((2, members, cdev, inner), BF16),
            pltpu.VMEM((members, hist_n, cdev, inner), BF16),
            pltpu.VMEM((members, hist_n, cdev, inner), BF16),
            pltpu.VMEM((members, hist_n, cdev, inner), BF16),
            pltpu.VMEM((members, heads, key_n), F32),
            pltpu.VMEM((members, hist_n, cdev, key_n), F32),
            dma((2 + 2 * members,)),
            dma(()),
            dma(()),
            dma((2, members)),
            dma((2, members)),
            dma((members, peers)),
            dma((members, peers)),
            dma((members, peers)),
            dma((members, peers)),
            dma(()),
            dma(()),
            dma(()),
            dma(()),
        ],
        compiler_params=pltpu.CompilerParams(
            collective_id=0, has_side_effects=True, vmem_limit_bytes=56 * 1024 * 1024
        ),
    )(
        candidates,
        cand_items.T,
        hist_keys,
        hist_values,
        hist_items,
        hist_buckets,
        lengths,
        norm_gain.reshape(1, width),
        in_weight,
        bias_table.T,
        out_weight,
    )
    return out.transpose(1, 0, 2)


def solution(mesh):
    in_specs = (
        P(("hist", "cand"), "fsdp", None),
        P(),
        P("fsdp", "hist", None),
        P("fsdp", "hist", None),
        P("fsdp", "hist"),
        P("fsdp", "hist"),
        P("fsdp"),
        P(),
        P(None, "fsdp"),
        P(),
        P(None, "fsdp"),
    )
    out_specs = P(("hist", "cand"), "fsdp", None)
    return jax.shard_map(
        functools.partial(body, mesh.shape["hist"], mesh.shape["cand"]),
        mesh=mesh,
        in_specs=in_specs,
        out_specs=out_specs,
        check_vma=False,
    )
```

```python
import functools

import jax
import jax.numpy as jnp
from jax import lax
from jax.experimental import pallas as pl
from jax.experimental.pallas import tpu as pltpu
from jax.sharding import PartitionSpec as P

MESH = pl.DeviceIdType.MESH
F32 = jnp.float32
BF16 = jnp.bfloat16
PIECES = 4
EARLY = 1
NT = (((1,), (1,)), ((), ()))


def half_silu(u):
    return u + u * jnp.tanh(u)


def layer_norm(x):
    c = x - jnp.mean(x, axis=-1, keepdims=True)
    return c * lax.rsqrt(jnp.mean(c * c, axis=-1, keepdims=True) + 1e-05)


def kernel(
    hist_n,
    cand_n,
    cand_ref,
    ids_ref,
    keys_hbm,
    vals_hbm,
    items_ref,
    buckets_ref,
    len_ref,
    gain_ref,
    inw_hbm,
    table_ref,
    outw_hbm,
    out_ref,
    inw,
    outw,
    keys,
    vals,
    x_buf,
    proj,
    psend,
    gq,
    part,
    recv,
    hbias,
    keep,
    loc_sem,
    a_send,
    a_recv,
    c_send,
    c_recv,
    d_send,
    d_recv,
    f_send,
    f_recv,
    o_send,
    o_recv,
    s_send,
    s_recv,
):
    hist = lax.axis_index("hist")
    cand = lax.axis_index("cand")
    fsdp = lax.axis_index("fsdp")
    other = 1 - fsdp
    cdev, members, width = cand_ref.shape
    heads, buckets = table_ref.shape
    inner = part.shape[-1]
    rows_own = members * cdev
    key_n = keys.shape[1]
    hd = inner // heads
    group = 256 // hd
    gcols = group * hd
    group_n = inner // gcols

    def remote(src, dst, ssem, rsem, **where):
        return pltpu.make_async_remote_copy(
            src_ref=src, dst_ref=dst, send_sem=ssem, recv_sem=rsem, device_id=where, device_id_type=MESH
        )

    loc = [pltpu.make_async_copy(inw_hbm, inw, loc_sem.at[0])]
    for m in range(members):
        loc.append(pltpu.make_async_copy(keys_hbm.at[m], keys.at[m], loc_sem.at[1 + 2 * m]))
        loc.append(pltpu.make_async_copy(vals_hbm.at[m], vals.at[m], loc_sem.at[2 + 2 * m]))
    w_copy = pltpu.make_async_copy(outw_hbm, outw.at[fsdp], loc_sem.at[1 + 2 * members])
    loc.insert(1, w_copy)

    barrier = pltpu.get_barrier_semaphore()
    peers = [lax.rem(hist + o, hist_n) for o in range(1, hist_n)]
    for peer in peers:
        pl.semaphore_signal(barrier, inc=1, device_id={"hist": peer}, device_id_type=MESH)
    pl.semaphore_signal(barrier, inc=1, device_id={"fsdp": other}, device_id_type=MESH)
    for copy in loc:
        copy.start()
    x3 = cand_ref[...].astype(F32)
    x = jnp.concatenate([x3[:, m, :] for m in range(members)], axis=0)
    x_buf[0] = (layer_norm(x) * gain_ref[...]).astype(BF16)
    pl.semaphore_wait(barrier, hist_n)

    a_copy = remote(x_buf.at[0], x_buf.at[1], a_send, a_recv, fsdp=other)
    a_copy.start()

    depth = inner // (2 * PIECES)
    first = lax.rem(hist, 2) * (inner // 2)
    pieces = [pl.ds(pl.multiple_of(first + k * depth, depth), depth) for k in range(PIECES)]
    o_copies = [
        remote(outw_hbm.at[r, :], outw.at[fsdp, r], o_send.at[k], o_recv.at[k], fsdp=other)
        for k, r in enumerate(pieces)
    ]
    sibling = hist + 1 - 2 * lax.rem(hist, 2)
    s_copies = [
        remote(outw.at[other, r], outw.at[other, r], s_send.at[k], s_recv.at[k], hist=sibling)
        for k, r in enumerate(pieces)
    ]
    for copy in o_copies[:EARLY]:
        copy.start()

    table = table_ref[...]
    t_hi = table.astype(BF16)
    rest = table - t_hi.astype(F32)
    t_mid = rest.astype(BF16)
    t_lo = (rest - t_mid.astype(F32)).astype(BF16)
    t3 = jnp.concatenate([t_hi, t_mid, t_lo], axis=0)
    for m in range(members):
        one_hot = (
            lax.broadcasted_iota(jnp.int32, (buckets, key_n), 0) == buckets_ref[m : m + 1, :]
        )
        b3 = jnp.dot(t3, one_hot.astype(F32).astype(BF16), preferred_element_type=F32)
        hbias[m] = 0.5 * (b3[:heads] + b3[heads : 2 * heads] + b3[2 * heads :])

    loc[0].wait()
    a_copy.wait()
    xs = x_buf[...].reshape(2 * rows_own, width)

    def project(p):
        u = 0.5 * jnp.dot(xs, inw[:, p * inner : (p + 1) * inner], preferred_element_type=F32)
        y = half_silu(u).astype(BF16)
        psend[p] = y[rows_own:].reshape(members, cdev, inner)
        copies = []
        for m in range(members):
            copy = remote(
                psend.at[p, m],
                proj.at[2 * fsdp + p, m],
                c_send.at[p, m],
                c_recv.at[p, m],
                fsdp=other,
            )
            copy.start()
            copies.append(copy)
        proj[2 * fsdp + p] = y[:rows_own].reshape(members, cdev, inner)
        return copies

    c0 = project(0)

    lane_ids = lax.broadcasted_iota(jnp.int32, (cdev, ids_ref.shape[1]), 1)
    row_ids = lax.broadcasted_iota(jnp.int32, (cdev, ids_ref.shape[1]), 0)
    place = hist * key_n + lax.broadcasted_iota(jnp.int32, (1, key_n), 1)
    for m in range(members):
        length = jnp.full((1, key_n), len_ref[m], jnp.int32)
        scale = jnp.where(place < length, 1.0 / (length.astype(F32) + 1.0), 0.0)

        def fill(h, carry):
            ids = ids_ref[pl.ds(fsdp * members + m, 1), :]
            mine = jnp.sum(
                jnp.where(lane_ids == row_ids + (h * cand_n + cand) * cdev, ids, 0),
                axis=1,
                keepdims=True,
            )
            keep[m, h] = jnp.where(mine != items_ref[m : m + 1, :], scale, 0.0)
            return carry

        lax.fori_loop(0, hist_n, fill, 0)

    d_copies = []
    for m in range(members):
        c0[m].wait()
        d_copies.append(
            [
                remote(
                    proj.at[2, m], gq.at[m, hist], d_send.at[m, o], d_recv.at[m, o], hist=peer
                )
                for o, peer in enumerate(peers)
            ]
        )
        for copy in d_copies[m]:
            copy.start()
        gq[m, hist] = proj[2, m]
    for copy in o_copies[EARLY:]:
        copy.start()
    c1 = project(1)

    hb = 4 if hist_n % 4 == 0 else 1
    rb = hb * cdev
    lane_head = lax.broadcasted_iota(jnp.int32, (rb, gcols), 1) // hd
    f_copies = []
    chunk = min(key_n, 512)
    for m in range(members):
        loc[2 + 2 * m].wait()
        loc[3 + 2 * m].wait()
        for copy in d_copies[m]:
            copy.wait()

        def step(i, carry):
            r = i // group_n
            g = i % group_n
            cols = pl.ds(pl.multiple_of(g * gcols, gcols), gcols)
            hs = pl.ds(r * hb, hb)
            q = gq[m, hs, :, cols].reshape(rb, gcols).astype(F32) * (0.5 * hd ** (-0.5))
            q4 = jnp.concatenate(
                [jnp.where(lane_head == h, q, 0.0).astype(BF16) for h in range(group)], axis=0
            )
            total = jnp.zeros((group * rb, gcols), F32)
            for j in range(0, key_n, chunk):
                s = lax.dot_general(
                    q4, keys[m, pl.ds(j, chunk), cols], NT, preferred_element_type=F32
                )
                kp = keep[m, hs, :, pl.ds(j, chunk)].reshape(rb, chunk)
                ws = []
                for h in range(group):
                    u = s[h * rb : (h + 1) * rb] + hbias[m, pl.ds(g * group + h, 1), pl.ds(j, chunk)]
                    ws.append((half_silu(u) * kp).astype(BF16))
                total += jnp.dot(
                    jnp.concatenate(ws, axis=0),
                    vals[m, pl.ds(j, chunk), cols],
                    preferred_element_type=F32,
                )
            summed = jnp.where(lane_head == 0, total[:rb], 0.0)
            for h in range(1, group):
                summed += jnp.where(lane_head == h, total[h * rb : (h + 1) * rb], 0.0)
            part[m, hs, :, cols] = summed.astype(BF16).reshape(hb, cdev, gcols)
            return carry

        lax.fori_loop(0, (hist_n // hb) * group_n, step, 0, unroll=2)
        for o, peer in enumerate(peers):
            copy = remote(
                part.at[m, peer], recv.at[m, hist], f_send.at[m, o], f_recv.at[m, o], hist=peer
            )
            copy.start()
            f_copies.append(copy)
        for k in range(m * PIECES // members, (m + 1) * PIECES // members):
            o_copies[k].wait()
            s_copies[k].start()

    for copy in c1:
        copy.wait()
    blk = (
        lax.broadcasted_iota(jnp.int32, (gcols, gcols), 0) // hd
        == lax.broadcasted_iota(jnp.int32, (gcols, gcols), 1) // hd
    ).astype(F32).astype(BF16)
    prod = proj[2].astype(F32).reshape(rows_own, inner) * proj[3].astype(F32).reshape(rows_own, inner)
    p_hi = prod.astype(BF16)
    p_lo = (prod - p_hi.astype(F32)).astype(BF16)
    dots = jnp.concatenate(
        [
            jnp.dot(p_hi[:, c : c + gcols], blk, preferred_element_type=F32)
            + jnp.dot(p_lo[:, c : c + gcols], blk, preferred_element_type=F32)
            for c in range(0, inner, gcols)
        ],
        axis=1,
    )
    lane = lax.broadcasted_iota(jnp.int32, (heads, inner), 1) // hd
    bias0 = jnp.sum(
        jnp.where(lax.broadcasted_iota(jnp.int32, (heads, inner), 0) == lane, table[:, 0:1], 0.0),
        axis=0,
        keepdims=True,
    )
    own = half_silu(dots * (0.5 * hd ** (-0.5)) + 0.5 * bias0)
    own = own * proj[1].astype(F32).reshape(rows_own, inner)
    inv = jnp.concatenate(
        [1.0 / (jnp.full((cdev, inner), len_ref[m], jnp.int32).astype(F32) + 1.0) for m in range(members)],
        axis=0,
    )
    attended = own * inv
    for m in range(members):
        recv[m, hist] = part[m, hist]
    for copy in f_copies:
        copy.wait()
    attended += jnp.sum(recv[...].astype(F32), axis=1).reshape(rows_own, inner)
    mixed = (layer_norm(attended) * proj[0].astype(F32).reshape(rows_own, inner)).astype(BF16)
    for copy in s_copies:
        copy.wait()
    w_copy.wait()
    full = jnp.concatenate(
        [jnp.dot(mixed, outw[f], preferred_element_type=F32) for f in range(2)], axis=1
    )
    x3 = cand_ref[...].astype(F32)
    x = jnp.concatenate([x3[:, m, :] for m in range(members)], axis=0)
    out_ref[...] = (x + full).astype(BF16).reshape(members, cdev, width)


def body(
    hist_n,
    cand_n,
    candidates,
    cand_items,
    hist_keys,
    hist_values,
    hist_items,
    hist_buckets,
    lengths,
    norm_gain,
    in_weight,
    bias_table,
    out_weight,
):
    cdev, members, width = candidates.shape
    key_n = hist_keys.shape[1]
    inner = out_weight.shape[0]
    heads = bias_table.shape[1]
    own = members * cdev
    vmem = pl.BlockSpec(memory_space=pltpu.VMEM)
    hbm = pl.BlockSpec(memory_space=pl.ANY)
    smem = pl.BlockSpec(memory_space=pltpu.SMEM)
    dma = pltpu.SemaphoreType.DMA
    peers = max(hist_n - 1, 1)
    out = pl.pallas_call(
        functools.partial(kernel, hist_n, cand_n),
        out_shape=jax.ShapeDtypeStruct((members, cdev, width), BF16),
        in_specs=[vmem, vmem, hbm, hbm, vmem, vmem, smem, vmem, hbm, vmem, hbm],
        out_specs=vmem,
        scratch_shapes=[
            pltpu.VMEM(in_weight.shape, BF16),
            pltpu.VMEM((2,) + out_weight.shape, BF16),
            pltpu.VMEM(hist_keys.shape, BF16),
            pltpu.VMEM(hist_values.shape, BF16),
            pltpu.VMEM((2, own, width), BF16),
            pltpu.VMEM((4, members, cdev, inner), BF16),
            pltpu.VMEM((2, members, cdev, inner), BF16),
            pltpu.VMEM((members, hist_n, cdev, inner), BF16),
            pltpu.VMEM((members, hist_n, cdev, inner), BF16),
            pltpu.VMEM((members, hist_n, cdev, inner), BF16),
            pltpu.VMEM((members, heads, key_n), F32),
            pltpu.VMEM((members, hist_n, cdev, key_n), F32),
            dma((2 + 2 * members,)),
            dma(()),
            dma(()),
            dma((2, members)),
            dma((2, members)),
            dma((members, peers)),
            dma((members, peers)),
            dma((members, peers)),
            dma((members, peers)),
            dma((PIECES,)),
            dma((PIECES,)),
            dma((PIECES,)),
            dma((PIECES,)),
        ],
        compiler_params=pltpu.CompilerParams(
            collective_id=0, has_side_effects=True, vmem_limit_bytes=56 * 1024 * 1024
        ),
    )(
        candidates,
        cand_items.T,
        hist_keys,
        hist_values,
        hist_items,
        hist_buckets,
        lengths,
        norm_gain.reshape(1, width),
        in_weight,
        bias_table.T,
        out_weight,
    )
    return out.transpose(1, 0, 2)


def solution(mesh):
    in_specs = (
        P(("hist", "cand"), "fsdp", None),
        P(),
        P("fsdp", "hist", None),
        P("fsdp", "hist", None),
        P("fsdp", "hist"),
        P("fsdp", "hist"),
        P("fsdp"),
        P(),
        P(None, "fsdp"),
        P(),
        P(None, "fsdp"),
    )
    out_specs = P(("hist", "cand"), "fsdp", None)
    return jax.shard_map(
        functools.partial(body, mesh.shape["hist"], mesh.shape["cand"]),
        mesh=mesh,
        in_specs=in_specs,
        out_specs=out_specs,
        check_vma=False,
    )
```

```python
import functools

import jax
import jax.numpy as jnp
from jax import lax
from jax.experimental import pallas as pl
from jax.experimental.pallas import tpu as pltpu
from jax.sharding import PartitionSpec as P

MESH = pl.DeviceIdType.MESH
F32 = jnp.float32
BF16 = jnp.bfloat16
PIECES = 4
EARLY = 1
NT = (((1,), (1,)), ((), ()))


def half_silu(u):
    return u + u * jnp.tanh(u)


def layer_norm(x):
    c = x - jnp.mean(x, axis=-1, keepdims=True)
    return c * lax.rsqrt(jnp.mean(c * c, axis=-1, keepdims=True) + 1e-05)


def kernel(
    hist_n,
    cand_n,
    cand_ref,
    ids_ref,
    keys_hbm,
    vals_hbm,
    items_ref,
    buckets_ref,
    len_ref,
    gain_ref,
    inw_hbm,
    table_ref,
    outw_hbm,
    out_ref,
    inw,
    outw,
    keys,
    vals,
    x_buf,
    proj,
    psend,
    gq,
    part,
    recv,
    hbias,
    keep,
    loc_sem,
    a_send,
    a_recv,
    c_send,
    c_recv,
    d_send,
    d_recv,
    f_send,
    f_recv,
    o_send,
    o_recv,
    s_send,
    s_recv,
):
    hist = lax.axis_index("hist")
    cand = lax.axis_index("cand")
    fsdp = lax.axis_index("fsdp")
    other = 1 - fsdp
    cdev, members, width = cand_ref.shape
    heads, buckets = table_ref.shape
    inner = part.shape[-1]
    rows_own = members * cdev
    key_n = keys.shape[1]
    hd = inner // heads
    group = 256 // hd
    gcols = group * hd
    group_n = inner // gcols

    def remote(src, dst, ssem, rsem, **where):
        return pltpu.make_async_remote_copy(
            src_ref=src, dst_ref=dst, send_sem=ssem, recv_sem=rsem, device_id=where, device_id_type=MESH
        )

    loc = [pltpu.make_async_copy(inw_hbm, inw, loc_sem.at[0])]
    for m in range(members):
        loc.append(pltpu.make_async_copy(keys_hbm.at[m], keys.at[m], loc_sem.at[1 + 2 * m]))
        loc.append(pltpu.make_async_copy(vals_hbm.at[m], vals.at[m], loc_sem.at[2 + 2 * m]))
    w_copy = pltpu.make_async_copy(outw_hbm, outw.at[fsdp], loc_sem.at[1 + 2 * members])
    loc.insert(1, w_copy)

    barrier = pltpu.get_barrier_semaphore()
    peers = [lax.rem(hist + o, hist_n) for o in range(1, hist_n)]
    for peer in peers:
        pl.semaphore_signal(barrier, inc=1, device_id={"hist": peer}, device_id_type=MESH)
    pl.semaphore_signal(barrier, inc=1, device_id={"fsdp": other}, device_id_type=MESH)
    for copy in loc:
        copy.start()
    x3 = cand_ref[...].astype(F32)
    x = jnp.concatenate([x3[:, m, :] for m in range(members)], axis=0)
    x_buf[0] = (layer_norm(x) * gain_ref[...]).astype(BF16)
    pl.semaphore_wait(barrier, hist_n)

    a_copy = remote(x_buf.at[0], x_buf.at[1], a_send, a_recv, fsdp=other)
    a_copy.start()

    depth = inner // (2 * PIECES)
    first = lax.rem(hist, 2) * (inner // 2)
    pair = lax.rem(hist // 2, 2)
    pieces = [
        pl.ds(pl.multiple_of(first + k * depth, depth), depth)
        for k in (pair, *range(2, PIECES), 1 - pair)
    ]
    o_copies = [
        remote(outw_hbm.at[r, :], outw.at[fsdp, r], o_send.at[k], o_recv.at[k], fsdp=other)
        for k, r in enumerate(pieces[:-1])
    ]
    x_copy = remote(
        outw.at[other, pieces[0]],
        outw.at[other, pieces[0]],
        o_send.at[PIECES - 1],
        o_recv.at[PIECES - 1],
        hist=hist + 2 - 4 * pair,
    )
    sibling = hist + 1 - 2 * lax.rem(hist, 2)
    s_copies = [
        remote(outw.at[other, r], outw.at[other, r], s_send.at[k], s_recv.at[k], hist=sibling)
        for k, r in enumerate(pieces)
    ]
    for copy in o_copies[:EARLY]:
        copy.start()

    table = table_ref[...]
    t_hi = table.astype(BF16)
    rest = table - t_hi.astype(F32)
    t_mid = rest.astype(BF16)
    t_lo = (rest - t_mid.astype(F32)).astype(BF16)
    t3 = jnp.concatenate([t_hi, t_mid, t_lo], axis=0)
    for m in range(members):
        one_hot = (
            lax.broadcasted_iota(jnp.int32, (buckets, key_n), 0) == buckets_ref[m : m + 1, :]
        )
        b3 = jnp.dot(t3, one_hot.astype(F32).astype(BF16), preferred_element_type=F32)
        hbias[m] = 0.5 * (b3[:heads] + b3[heads : 2 * heads] + b3[2 * heads :])

    loc[0].wait()
    a_copy.wait()
    xs = x_buf[...].reshape(2 * rows_own, width)

    def project(p):
        u = 0.5 * jnp.dot(xs, inw[:, p * inner : (p + 1) * inner], preferred_element_type=F32)
        y = half_silu(u).astype(BF16)
        psend[p] = y[rows_own:].reshape(members, cdev, inner)
        copies = []
        for m in range(members):
            copy = remote(
                psend.at[p, m],
                proj.at[2 * fsdp + p, m],
                c_send.at[p, m],
                c_recv.at[p, m],
                fsdp=other,
            )
            copy.start()
            copies.append(copy)
        proj[2 * fsdp + p] = y[:rows_own].reshape(members, cdev, inner)
        return copies

    c0 = project(0)

    lane_ids = lax.broadcasted_iota(jnp.int32, (cdev, ids_ref.shape[1]), 1)
    row_ids = lax.broadcasted_iota(jnp.int32, (cdev, ids_ref.shape[1]), 0)
    place = hist * key_n + lax.broadcasted_iota(jnp.int32, (1, key_n), 1)
    for m in range(members):
        length = jnp.full((1, key_n), len_ref[m], jnp.int32)
        scale = jnp.where(place < length, 1.0 / (length.astype(F32) + 1.0), 0.0)

        def fill(h, carry):
            ids = ids_ref[pl.ds(fsdp * members + m, 1), :]
            mine = jnp.sum(
                jnp.where(lane_ids == row_ids + (h * cand_n + cand) * cdev, ids, 0),
                axis=1,
                keepdims=True,
            )
            keep[m, h] = jnp.where(mine != items_ref[m : m + 1, :], scale, 0.0)
            return carry

        lax.fori_loop(0, hist_n, fill, 0)

    d_copies = []
    for m in range(members):
        c0[m].wait()
        d_copies.append(
            [
                remote(
                    proj.at[2, m], gq.at[m, hist], d_send.at[m, o], d_recv.at[m, o], hist=peer
                )
                for o, peer in enumerate(peers)
            ]
        )
        for copy in d_copies[m]:
            copy.start()
        gq[m, hist] = proj[2, m]
    for copy in o_copies[EARLY:]:
        copy.start()
    c1 = project(1)

    hb = 4 if hist_n % 4 == 0 else 1
    rb = hb * cdev
    lane_head = lax.broadcasted_iota(jnp.int32, (rb, gcols), 1) // hd
    f_copies = []
    chunk = min(key_n, 512)
    for m in range(members):
        loc[2 + 2 * m].wait()
        loc[3 + 2 * m].wait()
        for copy in d_copies[m]:
            copy.wait()
        if m == 0:
            o_copies[0].wait()
            x_copy.start()
            s_copies[0].start()

        def step(i, carry):
            r = i // group_n
            g = i % group_n
            cols = pl.ds(pl.multiple_of(g * gcols, gcols), gcols)
            hs = pl.ds(r * hb, hb)
            q = gq[m, hs, :, cols].reshape(rb, gcols).astype(F32) * (0.5 * hd ** (-0.5))
            q4 = jnp.concatenate(
                [jnp.where(lane_head == h, q, 0.0).astype(BF16) for h in range(group)], axis=0
            )
            total = jnp.zeros((group * rb, gcols), F32)
            for j in range(0, key_n, chunk):
                s = lax.dot_general(
                    q4, keys[m, pl.ds(j, chunk), cols], NT, preferred_element_type=F32
                )
                kp = keep[m, hs, :, pl.ds(j, chunk)].reshape(rb, chunk)
                ws = []
                for h in range(group):
                    u = s[h * rb : (h + 1) * rb] + hbias[m, pl.ds(g * group + h, 1), pl.ds(j, chunk)]
                    ws.append((half_silu(u) * kp).astype(BF16))
                total += jnp.dot(
                    jnp.concatenate(ws, axis=0),
                    vals[m, pl.ds(j, chunk), cols],
                    preferred_element_type=F32,
                )
            summed = jnp.where(lane_head == 0, total[:rb], 0.0)
            for h in range(1, group):
                summed += jnp.where(lane_head == h, total[h * rb : (h + 1) * rb], 0.0)
            part[m, hs, :, cols] = summed.astype(BF16).reshape(hb, cdev, gcols)
            return carry

        lax.fori_loop(0, (hist_n // hb) * group_n, step, 0, unroll=2)
        for o, peer in enumerate(peers):
            copy = remote(
                part.at[m, peer], recv.at[m, hist], f_send.at[m, o], f_recv.at[m, o], hist=peer
            )
            copy.start()
            f_copies.append(copy)
    for k in range(1, PIECES - 1):
        o_copies[k].wait()
        s_copies[k].start()
    x_copy.wait()
    s_copies[-1].start()
    for copy in c1:
        copy.wait()
    blk = (
        lax.broadcasted_iota(jnp.int32, (gcols, gcols), 0) // hd
        == lax.broadcasted_iota(jnp.int32, (gcols, gcols), 1) // hd
    ).astype(F32).astype(BF16)
    prod = proj[2].astype(F32).reshape(rows_own, inner) * proj[3].astype(F32).reshape(rows_own, inner)
    p_hi = prod.astype(BF16)
    p_lo = (prod - p_hi.astype(F32)).astype(BF16)
    dots = jnp.concatenate(
        [
            jnp.dot(p_hi[:, c : c + gcols], blk, preferred_element_type=F32)
            + jnp.dot(p_lo[:, c : c + gcols], blk, preferred_element_type=F32)
            for c in range(0, inner, gcols)
        ],
        axis=1,
    )
    lane = lax.broadcasted_iota(jnp.int32, (heads, inner), 1) // hd
    bias0 = jnp.sum(
        jnp.where(lax.broadcasted_iota(jnp.int32, (heads, inner), 0) == lane, table[:, 0:1], 0.0),
        axis=0,
        keepdims=True,
    )
    own = half_silu(dots * (0.5 * hd ** (-0.5)) + 0.5 * bias0)
    own = own * proj[1].astype(F32).reshape(rows_own, inner)
    inv = jnp.concatenate(
        [1.0 / (jnp.full((cdev, inner), len_ref[m], jnp.int32).astype(F32) + 1.0) for m in range(members)],
        axis=0,
    )
    attended = own * inv
    for m in range(members):
        recv[m, hist] = part[m, hist]
    for copy in f_copies:
        copy.wait()
    attended += jnp.sum(recv[...].astype(F32), axis=1).reshape(rows_own, inner)
    mixed = (layer_norm(attended) * proj[0].astype(F32).reshape(rows_own, inner)).astype(BF16)
    for copy in s_copies:
        copy.wait()
    w_copy.wait()
    full = jnp.concatenate(
        [jnp.dot(mixed, outw[f], preferred_element_type=F32) for f in range(2)], axis=1
    )
    x3 = cand_ref[...].astype(F32)
    x = jnp.concatenate([x3[:, m, :] for m in range(members)], axis=0)
    out_ref[...] = (x + full).astype(BF16).reshape(members, cdev, width)


def body(
    hist_n,
    cand_n,
    candidates,
    cand_items,
    hist_keys,
    hist_values,
    hist_items,
    hist_buckets,
    lengths,
    norm_gain,
    in_weight,
    bias_table,
    out_weight,
):
    cdev, members, width = candidates.shape
    key_n = hist_keys.shape[1]
    inner = out_weight.shape[0]
    heads = bias_table.shape[1]
    own = members * cdev
    vmem = pl.BlockSpec(memory_space=pltpu.VMEM)
    hbm = pl.BlockSpec(memory_space=pl.ANY)
    smem = pl.BlockSpec(memory_space=pltpu.SMEM)
    dma = pltpu.SemaphoreType.DMA
    peers = max(hist_n - 1, 1)
    out = pl.pallas_call(
        functools.partial(kernel, hist_n, cand_n),
        out_shape=jax.ShapeDtypeStruct((members, cdev, width), BF16),
        in_specs=[vmem, vmem, hbm, hbm, vmem, vmem, smem, vmem, hbm, vmem, hbm],
        out_specs=vmem,
        scratch_shapes=[
            pltpu.VMEM(in_weight.shape, BF16),
            pltpu.VMEM((2,) + out_weight.shape, BF16),
            pltpu.VMEM(hist_keys.shape, BF16),
            pltpu.VMEM(hist_values.shape, BF16),
            pltpu.VMEM((2, own, width), BF16),
            pltpu.VMEM((4, members, cdev, inner), BF16),
            pltpu.VMEM((2, members, cdev, inner), BF16),
            pltpu.VMEM((members, hist_n, cdev, inner), BF16),
            pltpu.VMEM((members, hist_n, cdev, inner), BF16),
            pltpu.VMEM((members, hist_n, cdev, inner), BF16),
            pltpu.VMEM((members, heads, key_n), F32),
            pltpu.VMEM((members, hist_n, cdev, key_n), F32),
            dma((2 + 2 * members,)),
            dma(()),
            dma(()),
            dma((2, members)),
            dma((2, members)),
            dma((members, peers)),
            dma((members, peers)),
            dma((members, peers)),
            dma((members, peers)),
            dma((PIECES,)),
            dma((PIECES,)),
            dma((PIECES,)),
            dma((PIECES,)),
        ],
        compiler_params=pltpu.CompilerParams(
            collective_id=0, has_side_effects=True, vmem_limit_bytes=56 * 1024 * 1024
        ),
    )(
        candidates,
        cand_items.T,
        hist_keys,
        hist_values,
        hist_items,
        hist_buckets,
        lengths,
        norm_gain.reshape(1, width),
        in_weight,
        bias_table.T,
        out_weight,
    )
    return out.transpose(1, 0, 2)


def solution(mesh):
    in_specs = (
        P(("hist", "cand"), "fsdp", None),
        P(),
        P("fsdp", "hist", None),
        P("fsdp", "hist", None),
        P("fsdp", "hist"),
        P("fsdp", "hist"),
        P("fsdp"),
        P(),
        P(None, "fsdp"),
        P(),
        P(None, "fsdp"),
    )
    out_specs = P(("hist", "cand"), "fsdp", None)
    return jax.shard_map(
        functools.partial(body, mesh.shape["hist"], mesh.shape["cand"]),
        mesh=mesh,
        in_specs=in_specs,
        out_specs=out_specs,
        check_vma=False,
    )
```
